128 devices in a mesh: dp: 32 (over z, y, x_hi), mp: 4 (over x_lo, core).
Axes of the slice: x: 4 (x_hi: 2, x_lo: 2; x = x_hi * 2 + x_lo), y: 4, z: 4, core: 2. Of those that a mesh axis runs over, the one named last changes fastest.
Arguments:
- train_acts: bfloat16 [128, 64, 4096], P('dp', None, 'mp')
- train_grads: bfloat16 [128, 64, 14336], P('dp', None, 'mp'), may hold values from -6 to 6
- train_lengths: int32 [128], P('dp'), may hold values from 1 to 64, as said below
- query_acts: bfloat16 [64, 8, 4096], P('dp', None, 'mp'), may hold values from -6 to 6
- query_grads: bfloat16 [64, 8, 14336], P('dp', None, 'mp'), may hold values from -6 to 6
- query_lengths: int32 [64], P('dp'), may hold values from 4 to 8, as said below
- proj_in: bfloat16 [64, 4096], P(None, 'mp'), may hold values from -0.09375 to 0.09375
- proj_out: bfloat16 [64, 14336], P(None, 'mp'), may hold values from -0.046875 to 0.046875
Outputs:
- precond: float32 [64, 4096], P(None, 'mp')
- scores: float32 [128, 64], P('dp', 'mp')
The draws below stay inside these ranges and needn't reach their ends.
Inputs may be any that keep to these rules, and one draw needn't show every extreme that they name: `train_lengths`: each training row uses at least one slot; some row uses all 64. `query_lengths`: some query uses all 8 slots and some uses exactly half of them.
All inputs are finite; a program needn't handle non-finite values.
Results may differ from the reference program's by a relative error of at most 0.0006.
Values sent between devices are 32-bit elements; how exact they have to be, the bound alone decides.
No kernel may reach another device: no remote copies, remote signals or barrier semaphores. Data moves between devices by JAX's collectives and lax.ppermute only.
A program may use at most 64 MiB of HBM per device.

```python
import math
import jax
import jax.numpy as jnp
from jax import lax

D = 4096
FF = 14336
R = 64
LEN = 64
QLEN = 8
ITERS = 4
ROWS = 128
QUERIES = 64


def draw_train_acts(key, part):
    key = jax.random.fold_in(key, 11)
    ramp = 1.0 + 2.0 * jnp.arange(ROWS, dtype=jnp.float32) / max(ROWS - 1, 1)
    values = jax.random.normal(key, (ROWS, LEN, D), jnp.float32) * ramp[:, None, None]
    values = jnp.clip(values, -8.0, 8.0)
    return values.astype(jnp.bfloat16)


def draw_train_lengths(key, part):
    key = jax.random.fold_in(key, 23)
    values = jax.random.randint(key, (ROWS,), 1, LEN + 1, dtype=jnp.int32)
    values = values.at[0].set(LEN)
    return values.at[ROWS - 1].set(1)


def draw_query_lengths(key, part):
    key = jax.random.fold_in(key, 37)
    values = jax.random.randint(key, (QUERIES,), QLEN // 2, QLEN + 1, dtype=jnp.int32)
    values = values.at[0].set(QLEN)
    return values.at[QUERIES - 1].set(QLEN // 2)


def levels(rng, extent, pieces, smallest, high):
    level, own = 1.0, jax.random.fold_in(rng, 6)
    for dim, parts in pieces:
        steps = jnp.exp(jax.random.uniform(jax.random.fold_in(own, dim), (parts,), jnp.float32, smallest / len(pieces), high / len(pieces)))
        level = level * jnp.repeat(steps, extent[dim] // parts).reshape([-1 if axis == dim else 1 for axis in range(len(extent))])
    return level


def bell_draw(own_key, extent, width, most, shards=(), held_as=jnp.bfloat16):
    level = levels(own_key, extent, shards, -0.22, 0.18) if shards else 1.0
    entries = jax.random.normal(own_key, extent, jnp.float32) * width * level
    return jnp.minimum(jnp.maximum(entries, -most), most).astype(held_as)


def setup_inputs(seed: int = 0) -> dict:
    key_of = jax.random.split(jax.random.key(seed), 9)
    train_acts = draw_train_acts(jax.random.fold_in(key_of[8], 71), 0)
    train_grads = bell_draw(key_of[1], (ROWS, LEN, FF), 1.0, 6.0, ((0, 32), (2, 4)))
    train_lengths = draw_train_lengths(jax.random.fold_in(key_of[8], 71), 0)
    query_acts = bell_draw(key_of[3], (QUERIES, QLEN, D), 1.0, 6.0, ((0, 32), (2, 4)))
    query_grads = bell_draw(key_of[4], (QUERIES, QLEN, FF), 1.0, 6.0, ((0, 32), (2, 4)))
    query_lengths = draw_query_lengths(jax.random.fold_in(key_of[8], 71), 0)
    proj_in = bell_draw(key_of[6], (R, D), D ** -0.5, 0.09375, ((1, 4),))
    proj_out = bell_draw(key_of[7], (R, FF), FF ** -0.5, 0.046875, ((1, 4),))
    return {"train_acts": train_acts, "train_grads": train_grads, "train_lengths": train_lengths, "query_acts": query_acts, "query_grads": query_grads, "query_lengths": query_lengths, "proj_in": proj_in, "proj_out": proj_out}


damping = 0.5
epsilon = 1e-06

def reference(train_acts, train_grads, train_lengths, query_acts, query_grads, query_lengths, proj_in, proj_out):
    highest = lax.Precision.HIGHEST
    train_in = jnp.dot(train_acts.reshape(-1, D), proj_in.T, preferred_element_type=jnp.float32).reshape(ROWS, LEN, R)
    train_out = jnp.dot(train_grads.reshape(-1, FF), proj_out.T, preferred_element_type=jnp.float32).reshape(ROWS, LEN, R)
    query_in = jnp.dot(query_acts.reshape(-1, D), proj_in.T, preferred_element_type=jnp.float32).reshape(QUERIES, QLEN, R)
    query_out = jnp.dot(query_grads.reshape(-1, FF), proj_out.T, preferred_element_type=jnp.float32).reshape(QUERIES, QLEN, R)
    token_mask = (jnp.arange(LEN, dtype=jnp.int32)[None, :] < train_lengths[:, None]).astype(jnp.float32)
    features = jnp.einsum('rti,rtj->rij', train_out * token_mask[:, :, None], train_in, precision=highest)
    features = features.reshape(ROWS, R * R) / math.sqrt(LEN)
    query_mask = (jnp.arange(QLEN, dtype=jnp.int32)[None, :] < query_lengths[:, None]).astype(jnp.float32)
    qfeatures = jnp.einsum('qti,qtj->qij', query_out * query_mask[:, :, None], query_in, precision=highest)
    qfeatures = qfeatures.reshape(QUERIES, R * R) / math.sqrt(QLEN)
    damp_value = damping * jnp.sum(features * features) / (ROWS * R * R) + epsilon
    solution = jnp.zeros_like(qfeatures)
    residual = qfeatures
    direction = qfeatures
    norm_now = lax.optimization_barrier(jnp.sum(residual * residual, axis=1))
    for step in range(ITERS):
        row_values = jnp.dot(features, direction.T, precision=highest)
        operator_image = damp_value * direction + jnp.dot(row_values.T, features, precision=highest) / ROWS
        curvature = lax.optimization_barrier(jnp.sum(direction * operator_image, axis=1))
        step_size = norm_now / curvature
        solution = solution + step_size[:, None] * direction
        residual = residual - step_size[:, None] * operator_image
        norm_next = lax.optimization_barrier(jnp.sum(residual * residual, axis=1))
        direction = residual + (norm_next / norm_now)[:, None] * direction
        norm_now = norm_next
    scores = jnp.dot(features, solution.T, precision=highest)
    return (solution, scores)
```

```python
import math

import jax
import jax.numpy as jnp
from jax import lax
from jax.experimental import pallas as pl
from jax.experimental.pallas import tpu as pltpu
from jax.sharding import PartitionSpec as P

ITERS = 4
DAMPING = 0.5
EPSILON = 1e-06
VMEM = 48 * 2**20
NZ, NY, NX = 4, 4, 2

NT = (((1,), (1,)), ((), ()))
NN = (((1,), (0,)), ((), ()))
TN = (((0,), (0,)), ((), ()))


def dot(a, b, dims):
    return lax.dot_general(
        a, b, dims, precision=lax.Precision.HIGHEST, preferred_element_type=jnp.float32
    )


def project_kernel(ta, tg, qa, qg, pi, po, own, to1, to2, to3,
                   ta_v, tg_v, qa_v, qg_v, pi_v, po_v, out_t, sems):
    copies = []
    for i, (src, dst) in enumerate(((pi, pi_v), (ta, ta_v), (qa, qa_v), (po, po_v), (qg, qg_v))):
        copies.append(pltpu.make_async_copy(src, dst, sems.at[i]))
    rows = tg.shape[0]
    for r in range(rows):
        copies.append(pltpu.make_async_copy(tg.at[r], tg_v.at[r], sems.at[5 + r]))
    for c in copies:
        c.start()
    me = lax.axis_index("mp")
    outs = (own, to1, to2, to3)

    def mm(a, b):
        return lax.dot_general(a, b, NT, preferred_element_type=jnp.float32)

    copies[0].wait()
    copies[1].wait()
    copies[2].wait()
    weights = pi_v[...]
    train_in = mm(ta_v[...].reshape(-1, ta_v.shape[2]), weights).T
    query_in = mm(qa_v[...], weights)
    for o in outs:
        o[0:64, :] = train_in[:, 0:128]
        o[80:144, :] = train_in[:, 128:256]
    copies[3].wait()
    copies[4].wait()
    weights = po_v[...]
    query_out = mm(qg_v[...], weights)
    queries = jnp.concatenate([query_in, query_out], axis=1)
    for o in outs:
        o[160:176, :] = queries
    for r in range(0, rows, 2):
        copies[5 + r].wait()
        copies[6 + r].wait()
        pair = mm(tg_v[r : r + 2].reshape(-1, tg_v.shape[2]), weights).T
        out_t[:, 64 * r : 64 * r + 128] = pair
    for k, o in enumerate(outs):
        quarter = out_t[pl.ds(pl.multiple_of((me ^ k) * 16, 16), 16), :]
        o[64:80, :] = quarter[:, 0:128]
        o[144:160, :] = quarter[:, 128:256]


def features_kernel(tl, ql, p0, p1, p2, p3, feats, scr, qscr):
    me = lax.axis_index("mp")
    x = (p0[...] + p1[...]) + (p2[...] + p3[...])
    lane = lax.broadcasted_iota(jnp.int32, (16, 128), 1)
    low = lax.broadcasted_iota(jnp.int32, (8, 128), 1) < 64
    for pair in range(2):
        base = 80 * pair
        inn = x[base : base + 64]
        out = x[base + 64 : base + 80]
        first = jnp.where(lane < tl[2 * pair], jnp.where(lane < 64, out, 0.0), 0.0)
        second = jnp.where(lane < 64 + tl[2 * pair + 1], jnp.where(lane >= 64, out, 0.0), 0.0)
        left = jnp.concatenate([first, second], axis=0)
        right = jnp.concatenate([inn, inn], axis=0)
        scr[32 * pair : 32 * pair + 32, :] = dot(left, right, NT)
    for r in range(4):
        even = scr[pl.ds(16 * r, 8, stride=2), :]
        odd = scr[pl.ds(16 * r + 1, 8, stride=2), :]
        feats[8 * r : 8 * r + 8, :] = jnp.where(low, even, odd) * 0.125
    q = x[160:176]
    slot = lax.broadcasted_iota(jnp.int32, (16, 64), 0)
    qin = q[:, 0:64]
    qout = q[:, 64:128]
    right = jnp.concatenate([qin, qin], axis=1)
    for r in range(2):
        keep = (slot >= 8 * r) & (slot < 8 * r + ql[r])
        qscr[64 * r : 64 * r + 64, :] = dot(jnp.where(keep, qout, 0.0), right, TN)
    for r in range(2):
        scr[0:16, :] = qscr[pl.ds(pl.multiple_of(64 * r + me * 16, 16), 16), :]
        even = scr[pl.ds(0, 8, stride=2), :]
        odd = scr[pl.ds(1, 8, stride=2), :]
        feats[32 + 8 * r : 40 + 8 * r, :] = jnp.where(low, even, odd) * (1.0 / math.sqrt(8.0))


def gram_kernel(y0, y1, y2, y3, part, fq, fs, qs):
    dp = lax.axis_index("dp")
    mz, my, mx = dp // (NY * NX), (dp // NX) % NY, dp % NX
    for j, ref in enumerate((y0, y1, y2, y3)):
        for k in range(NZ):
            for e in range(NX):
                slot = ((mz + NZ - k) % NZ * NY + (my + NY - j) % NY) * NX + (mx ^ e)
                at = 48 * (2 * k + e)
                fs[pl.ds(pl.multiple_of(slot * 32, 32), 32), :] = ref[at : at + 32, :]
                qs[pl.ds(pl.multiple_of(slot * 16, 16), 16), :] = ref[at + 32 : at + 48, :]
    total = jnp.zeros((192, 128), jnp.float32)
    squares = jnp.zeros((64, 128), jnp.float32)
    for a in range(8):
        f = fs[pl.ds(a, 128, stride=8), :]
        q = qs[pl.ds(a, 64, stride=8), :]
        fq[a, 0:128, :] = f
        fq[a, 128:192, :] = q
        total += dot(jnp.concatenate([f, q], axis=0), f, NT)
        squares += q * q
    part[0:192, :] = total
    norms = dot(jnp.ones((8, 128), jnp.float32), squares, NT)
    part[192:200, :] = jnp.concatenate([norms, norms], axis=1)


def solve_kernel(p0, p1, p2, p3, fq, precond, scores, ys):
    dp = lax.axis_index("dp")
    me = lax.axis_index("mp")
    x = (p0[...] + p1[...]) + (p2[...] + p3[...])
    gram = x[0:128]
    cross = x[128:192]
    row = lax.broadcasted_iota(jnp.int32, (64, 128), 0)
    col = lax.broadcasted_iota(jnp.int32, (64, 128), 1)
    norm_q = jnp.sum(jnp.where(row == col, jnp.broadcast_to(x[192:193], (64, 128)), 0.0),
                     axis=1, keepdims=True)
    grow = lax.broadcasted_iota(jnp.int32, (128, 128), 0)
    gcol = lax.broadcasted_iota(jnp.int32, (128, 128), 1)
    trace = jnp.sum(jnp.where(grow == gcol, gram, 0.0))
    damp = DAMPING * trace / (128 * 64 * 64) + EPSILON
    inv_rows = 1.0 / 128

    def inner(alpha, w, y):
        return alpha * (alpha * norm_q + jnp.sum(cross * w, axis=1, keepdims=True)) + jnp.sum(
            w * y, axis=1, keepdims=True
        )

    ra, rw, ry = jnp.ones((64, 1), jnp.float32), jnp.zeros((64, 128), jnp.float32), cross
    da, dw, dy = ra, rw, ry
    za, zw, zy = jnp.zeros((64, 1), jnp.float32), rw, rw
    rr = norm_q
    dd = norm_q
    for step in range(ITERS):
        curvature = damp * dd + jnp.sum(dy * dy, axis=1, keepdims=True) * inv_rows
        size = rr / curvature
        za, zw, zy = za + size * da, zw + size * dw, zy + size * dy
        if step == ITERS - 1:
            break
        iy = damp * dy + dot(dy, gram, NN) * inv_rows
        ra = ra - size * (damp * da)
        rw = rw - size * (damp * dw + dy * inv_rows)
        ry = ry - size * iy
        new = inner(ra, rw, ry)
        ratio = new / rr
        da, dw, dy = ra + ratio * da, rw + ratio * dw, ry + ratio * dy
        rr = new
        dd = inner(da, dw, dy)
    for a in range(8):
        precond[:, 128 * a : 128 * a + 128] = za * fq[a, 128:192, :] + dot(zw, fq[a, 0:128, :], NN)
    ys[...] = zy
    mine = ys[pl.ds(pl.multiple_of(me * 16, 16), 16), :]
    pick = (lax.broadcasted_iota(jnp.int32, (8, 128), 1)
            == lax.broadcasted_iota(jnp.int32, (8, 128), 0) + 4 * dp).astype(jnp.float32)
    scores[...] = dot(pick, mine, NT)[0:4]


def whole(n):
    return [pl.BlockSpec(memory_space=pltpu.VMEM)] * n


def call(kernel, shapes, in_specs, scratch, name):
    return pl.pallas_call(
        kernel,
        out_shape=[jax.ShapeDtypeStruct(s, jnp.float32) for s in shapes],
        in_specs=in_specs,
        out_specs=whole(len(shapes)),
        scratch_shapes=scratch,
        compiler_params=pltpu.CompilerParams(vmem_limit_bytes=VMEM),
        name=name,
    )


def dp_index(z, y, x):
    return (z * NY + y) * NX + x


def shift(dz, dy, dx):
    return [
        (dp_index(z, y, x), dp_index((z + dz) % NZ, (y + dy) % NY, (x + dx) % NX))
        for z in range(NZ)
        for y in range(NY)
        for x in range(NX)
    ]


def local(train_acts, train_grads, train_lengths, query_acts, query_grads, query_lengths,
          proj_in, proj_out):
    d, ff = proj_in.shape[1], proj_out.shape[1]
    bf = jnp.bfloat16
    own, *others = call(
        project_kernel,
        [(176, 128)] * 4,
        [pl.BlockSpec(memory_space=pl.ANY)] * 6,
        [
            pltpu.VMEM((4, 64, d), bf),
            pltpu.VMEM((4, 64, ff), bf),
            pltpu.VMEM((16, d), bf),
            pltpu.VMEM((16, ff), bf),
            pltpu.VMEM((64, d), bf),
            pltpu.VMEM((64, ff), bf),
            pltpu.VMEM((64, 256), jnp.float32),
            pltpu.SemaphoreType.DMA((9,)),
        ],
        "project",
    )(train_acts, train_grads, query_acts.reshape(16, d), query_grads.reshape(16, ff),
      proj_in, proj_out)
    got = [
        lax.ppermute(o, "mp", [(i, i ^ k) for i in range(4)]) for k, o in zip((1, 2, 3), others)
    ]
    smem = pl.BlockSpec(memory_space=pltpu.SMEM)
    (tiles,) = call(
        features_kernel,
        [(48, 128)],
        [smem, smem] + whole(4),
        [pltpu.VMEM((64, 128), jnp.float32), pltpu.VMEM((128, 128), jnp.float32)],
        "features",
    )(train_lengths, query_lengths, own, *got)
    tiles = jnp.concatenate([tiles, lax.ppermute(tiles, "dp", shift(0, 0, 1))], axis=0)
    tiles = jnp.concatenate(
        [tiles] + [lax.ppermute(tiles, "dp", shift(k, 0, 0)) for k in range(1, NZ)], axis=0
    )
    planes = [tiles] + [lax.ppermute(tiles, "dp", shift(0, k, 0)) for k in range(1, NY)]
    part, fq = call(
        gram_kernel,
        [(200, 128), (8, 192, 128)],
        whole(4),
        [pltpu.VMEM((1024, 128), jnp.float32), pltpu.VMEM((512, 128), jnp.float32)],
        "gram",
    )(*planes)
    got = [lax.ppermute(part, "mp", [(i, i ^ k) for i in range(4)]) for k in (1, 2, 3)]
    precond, scores = call(
        solve_kernel,
        [(64, 1024), (4, 16)],
        whole(5),
        [pltpu.VMEM((64, 128), jnp.float32)],
        "solve",
    )(part, *got, fq)
    return precond, scores


def solution(mesh):
    in_specs = (
        P("dp", None, "mp"),
        P("dp", None, "mp"),
        P("dp"),
        P("dp", None, "mp"),
        P("dp", None, "mp"),
        P("dp"),
        P(None, "mp"),
        P(None, "mp"),
    )
    out_specs = (P(None, "mp"), P("dp", "mp"))
    return jax.shard_map(local, mesh=mesh, in_specs=in_specs, out_specs=out_specs, check_vma=False)
```

```python
import math

import jax
import jax.numpy as jnp
from jax import lax
from jax.experimental import pallas as pl
from jax.experimental.pallas import tpu as pltpu
from jax.sharding import PartitionSpec as P

ITERS = 4
DAMPING = 0.5
EPSILON = 1e-06
VMEM = 48 * 2**20
NZ, NY, NX = 4, 4, 2

NT = (((1,), (1,)), ((), ()))
NN = (((1,), (0,)), ((), ()))
TN = (((0,), (0,)), ((), ()))


def dot(a, b, dims):
    return lax.dot_general(
        a, b, dims, precision=lax.Precision.HIGHEST, preferred_element_type=jnp.float32
    )


def project_kernel(ta, tg, qa, qg, pi, po, own, to1, to2, to3,
                   ta_v, tg_v, qa_v, qg_v, pi_v, po_v, out_t, sems):
    copies = []
    for i, (src, dst) in enumerate(((pi, pi_v), (ta, ta_v), (qa, qa_v), (po, po_v), (qg, qg_v))):
        copies.append(pltpu.make_async_copy(src, dst, sems.at[i]))
    rows = tg.shape[0]
    for r in range(rows):
        copies.append(pltpu.make_async_copy(tg.at[r], tg_v.at[r], sems.at[5 + r]))
    for c in copies:
        c.start()
    me = lax.axis_index("mp")
    outs = (own, to1, to2, to3)

    def mm(a, b):
        return lax.dot_general(a, b, NT, preferred_element_type=jnp.float32)

    copies[0].wait()
    copies[1].wait()
    copies[2].wait()
    weights = pi_v[...]
    train_in = mm(ta_v[...].reshape(-1, ta_v.shape[2]), weights).T
    query_in = mm(qa_v[...], weights)
    for o in outs:
        o[0:64, :] = train_in[:, 0:128]
        o[80:144, :] = train_in[:, 128:256]
    copies[3].wait()
    copies[4].wait()
    weights = po_v[...]
    query_out = mm(qg_v[...], weights)
    queries = jnp.concatenate([query_in, query_out], axis=1)
    for o in outs:
        o[160:176, :] = queries
    for r in range(0, rows, 2):
        copies[5 + r].wait()
        copies[6 + r].wait()
        pair = mm(tg_v[r : r + 2].reshape(-1, tg_v.shape[2]), weights).T
        out_t[:, 64 * r : 64 * r + 128] = pair
    for k, o in enumerate(outs):
        quarter = out_t[pl.ds(pl.multiple_of((me ^ k) * 16, 16), 16), :]
        o[64:80, :] = quarter[:, 0:128]
        o[144:160, :] = quarter[:, 128:256]


def features_kernel(tl, ql, p0, p1, p2, p3, feats, scr, qscr):
    me = lax.axis_index("mp")
    x = (p0[...] + p1[...]) + (p2[...] + p3[...])
    lane = lax.broadcasted_iota(jnp.int32, (16, 128), 1)
    low = lax.broadcasted_iota(jnp.int32, (8, 128), 1) < 64
    for pair in range(2):
        base = 80 * pair
        inn = x[base : base + 64]
        out = x[base + 64 : base + 80]
        first = jnp.where(lane < tl[2 * pair], jnp.where(lane < 64, out, 0.0), 0.0)
        second = jnp.where(lane < 64 + tl[2 * pair + 1], jnp.where(lane >= 64, out, 0.0), 0.0)
        left = jnp.concatenate([first, second], axis=0)
        right = jnp.concatenate([inn, inn], axis=0)
        scr[32 * pair : 32 * pair + 32, :] = dot(left, right, NT)
    for r in range(4):
        even = scr[pl.ds(16 * r, 8, stride=2), :]
        odd = scr[pl.ds(16 * r + 1, 8, stride=2), :]
        feats[8 * r : 8 * r + 8, :] = jnp.where(low, even, odd) * 0.125
    q = x[160:176]
    slot = lax.broadcasted_iota(jnp.int32, (16, 64), 0)
    qin = q[:, 0:64]
    qout = q[:, 64:128]
    right = jnp.concatenate([qin, qin], axis=1)
    for r in range(2):
        keep = (slot >= 8 * r) & (slot < 8 * r + ql[r])
        qscr[64 * r : 64 * r + 64, :] = dot(jnp.where(keep, qout, 0.0), right, TN)
    for r in range(2):
        scr[0:16, :] = qscr[pl.ds(pl.multiple_of(64 * r + me * 16, 16), 16), :]
        even = scr[pl.ds(0, 8, stride=2), :]
        odd = scr[pl.ds(1, 8, stride=2), :]
        feats[32 + 8 * r : 40 + 8 * r, :] = jnp.where(low, even, odd) * (1.0 / math.sqrt(8.0))


def gram_kernel(tiles, part, fq, fs, qs):
    mx = lax.axis_index("dp") % NX
    for s in range(NZ * NY):
        for e in range(NX):
            slot = NX * s + e
            at = 48 * (NX * s + e)
            fs[pl.ds(pl.multiple_of(slot * 32, 32), 32), :] = tiles[at : at + 32, :]
            qs[pl.ds(pl.multiple_of(slot * 16, 16), 16), :] = tiles[at + 32 : at + 48, :]
    total = jnp.zeros((192, 128), jnp.float32)
    squares = jnp.zeros((64, 128), jnp.float32)
    for a in range(8):
        f = fs[pl.ds(a, 128, stride=8), :]
        q = qs[pl.ds(a, 64, stride=8), :]
        fq[a, 0:128, :] = f
        fq[a, 128:192, :] = q
        total += dot(jnp.concatenate([f, q], axis=0), f, NT)
        squares += q * q
    ones = jnp.ones((8, 128), jnp.float32)
    row = lax.broadcasted_iota(jnp.int32, (64, 64), 0)
    col = lax.broadcasted_iota(jnp.int32, (64, 64), 1)
    both = jnp.where(row >= col, total[64:128, 64:128], total[0:64, 0:64])
    part[0:64, :] = jnp.concatenate([total[64:128, 0:64], both], axis=1)
    part[64:128, :] = total[128:192]
    diag = jnp.sum(jnp.where(row == col, total[0:64, 0:64], 0.0), axis=0, keepdims=True)
    norms = dot(ones, squares, NT)
    part[128:136, :] = jnp.concatenate([norms, jnp.broadcast_to(diag, (8, 64))], axis=1)


def solve_kernel(p0, p1, p2, p3, fq, precond, scores, ys):
    dp = lax.axis_index("dp")
    me = lax.axis_index("mp")
    x = (p0[...] + p1[...]) + (p2[...] + p3[...])
    row = lax.broadcasted_iota(jnp.int32, (64, 64), 0)
    col = lax.broadcasted_iota(jnp.int32, (64, 64), 1)
    both = x[0:64, 64:128]
    flip = both.T
    diag = jnp.broadcast_to(x[128:129, 64:128], (64, 64))
    upper = jnp.where(row < col, both, jnp.where(row > col, flip, diag))
    lower = jnp.where(row < col, flip, both)
    corner = x[0:64, 0:64]
    gram = jnp.concatenate(
        [jnp.concatenate([upper, corner.T], axis=1), jnp.concatenate([corner, lower], axis=1)],
        axis=0,
    )
    cross = x[64:128]
    norm_q = jnp.sum(jnp.where(row == col, jnp.broadcast_to(x[128:129, 0:64], (64, 64)), 0.0),
                     axis=1, keepdims=True)
    grow = lax.broadcasted_iota(jnp.int32, (128, 128), 0)
    gcol = lax.broadcasted_iota(jnp.int32, (128, 128), 1)
    trace = jnp.sum(jnp.where(grow == gcol, gram, 0.0))
    damp = DAMPING * trace / (128 * 64 * 64) + EPSILON
    inv_rows = 1.0 / 128

    def inner(alpha, w, y):
        return alpha * (alpha * norm_q + jnp.sum(cross * w, axis=1, keepdims=True)) + jnp.sum(
            w * y, axis=1, keepdims=True
        )

    ra, rw, ry = jnp.ones((64, 1), jnp.float32), jnp.zeros((64, 128), jnp.float32), cross
    da, dw, dy = ra, rw, ry
    za, zw, zy = jnp.zeros((64, 1), jnp.float32), rw, rw
    rr = norm_q
    dd = norm_q
    for step in range(ITERS):
        curvature = damp * dd + jnp.sum(dy * dy, axis=1, keepdims=True) * inv_rows
        size = rr / curvature
        za, zw, zy = za + size * da, zw + size * dw, zy + size * dy
        if step == ITERS - 1:
            break
        iy = damp * dy + dot(dy, gram, NN) * inv_rows
        ra = ra - size * (damp * da)
        rw = rw - size * (damp * dw + dy * inv_rows)
        ry = ry - size * iy
        new = inner(ra, rw, ry)
        ratio = new / rr
        da, dw, dy = ra + ratio * da, rw + ratio * dw, ry + ratio * dy
        rr = new
        dd = inner(da, dw, dy)
    for a in range(8):
        precond[:, 128 * a : 128 * a + 128] = za * fq[a, 128:192, :] + dot(zw, fq[a, 0:128, :], NN)
    ys[...] = zy
    mine = ys[pl.ds(pl.multiple_of(me * 16, 16), 16), :]
    pick = (lax.broadcasted_iota(jnp.int32, (8, 128), 1)
            == lax.broadcasted_iota(jnp.int32, (8, 128), 0) + 4 * dp).astype(jnp.float32)
    scores[...] = dot(pick, mine, NT)[0:4]


def whole(n):
    return [pl.BlockSpec(memory_space=pltpu.VMEM)] * n


def call(kernel, shapes, in_specs, scratch, name):
    return pl.pallas_call(
        kernel,
        out_shape=[jax.ShapeDtypeStruct(s, jnp.float32) for s in shapes],
        in_specs=in_specs,
        out_specs=whole(len(shapes)),
        scratch_shapes=scratch,
        compiler_params=pltpu.CompilerParams(vmem_limit_bytes=VMEM),
        name=name,
    )


def local(train_acts, train_grads, train_lengths, query_acts, query_grads, query_lengths,
          proj_in, proj_out):
    d, ff = proj_in.shape[1], proj_out.shape[1]
    bf = jnp.bfloat16
    own, *others = call(
        project_kernel,
        [(176, 128)] * 4,
        [pl.BlockSpec(memory_space=pltpu.HBM)] * 6,
        [
            pltpu.VMEM((4, 64, d), bf),
            pltpu.VMEM((4, 64, ff), bf),
            pltpu.VMEM((16, d), bf),
            pltpu.VMEM((16, ff), bf),
            pltpu.VMEM((64, d), bf),
            pltpu.VMEM((64, ff), bf),
            pltpu.VMEM((64, 256), jnp.float32),
            pltpu.SemaphoreType.DMA((9,)),
        ],
        "project",
    )(*(pltpu.with_memory_space_constraint(a, pltpu.HBM)
        for a in (train_acts, train_grads, query_acts.reshape(16, d),
                  query_grads.reshape(16, ff), proj_in, proj_out)))
    got = [
        lax.ppermute(o, "mp", [(i, i ^ k) for i in range(4)]) for k, o in zip((1, 2, 3), others)
    ]
    dp = NZ * NY * NX
    swap_x = [(i, i ^ 1) for i in range(dp)]
    planes = [list(range(x, dp, NX)) for x in range(NX)]
    smem = pl.BlockSpec(memory_space=pltpu.SMEM)
    (tiles,) = call(
        features_kernel,
        [(48, 128)],
        [smem, smem] + whole(4),
        [pltpu.VMEM((64, 128), jnp.float32), pltpu.VMEM((128, 128), jnp.float32)],
        "features",
    )(train_lengths, query_lengths, own, *got)
    tiles = jnp.broadcast_to(tiles[None], (dp, 48, 128))
    tiles = lax.all_to_all(tiles, "dp", 0, 0, tiled=True)
    part, fq = call(
        gram_kernel,
        [(136, 128), (8, 192, 128)],
        whole(1),
        [pltpu.VMEM((1024, 128), jnp.float32), pltpu.VMEM((512, 128), jnp.float32)],
        "gram",
    )(tiles.reshape(-1, 128))
    got = [lax.ppermute(part, "mp", [(i, i ^ k) for i in range(4)]) for k in (1, 2, 3)]
    precond, scores = call(
        solve_kernel,
        [(64, 1024), (4, 16)],
        whole(5),
        [pltpu.VMEM((64, 128), jnp.float32)],
        "solve",
    )(part, *got, fq)
    return precond, scores


def solution(mesh):
    in_specs = (
        P("dp", None, "mp"),
        P("dp", None, "mp"),
        P("dp"),
        P("dp", None, "mp"),
        P("dp", None, "mp"),
        P("dp"),
        P(None, "mp"),
        P(None, "mp"),
    )
    out_specs = (P(None, "mp"), P("dp", "mp"))
    return jax.shard_map(local, mesh=mesh, in_specs=in_specs, out_specs=out_specs, check_vma=False)
```

```python
import math

import jax
import jax.numpy as jnp
from jax import lax
from jax.experimental import pallas as pl
from jax.experimental.pallas import tpu as pltpu
from jax.sharding import PartitionSpec as P

ITERS = 4
DAMPING = 0.5
EPSILON = 1e-06
ROWS, QUERIES, RANK, LEN, QLEN = 128, 64, 64, 64, 8
VMEM = 48 * 2**20

NT = (((1,), (1,)), ((), ()))
NN = (((1,), (0,)), ((), ()))
TN = (((0,), (0,)), ((), ()))


def mm(a, b, dims):
    return lax.dot_general(a, b, dims, preferred_element_type=jnp.float32)


def split(x):
    high = x.astype(jnp.bfloat16)
    return high, (x - high.astype(jnp.float32)).astype(jnp.bfloat16)


def project_kernel(ta, tg, qa, qg, pi, po, keep, give, a_v, g_v, pi_v, po_v, out_t, sems):
    rows, length, ff = tg.shape
    slots = rows * length
    half = ff // 2
    count = iter(range(32))

    def load(src, dst):
        return pltpu.make_async_copy(src, dst, sems.at[next(count)])

    groups = [[load(pi, pi_v), load(qa, a_v.at[slots : slots + 16])]]
    for r in range(rows):
        groups[0].append(load(ta.at[r], a_v.at[length * r : length * (r + 1)]))
    for c in range(2):
        cols = pl.ds(half * c, half)
        group = [load(po.at[:, cols], po_v.at[:, cols]),
                 load(qg.at[:, cols], g_v.at[slots : slots + 16, cols])]
        for r in range(rows):
            group.append(load(tg.at[r, :, cols], g_v.at[length * r : length * (r + 1), cols]))
        groups.append(group)
    for group in groups:
        for c in group:
            c.start()
    me = lax.axis_index("mp")
    for c in groups[0]:
        c.wait()
    inn = mm(a_v[...], pi_v[...], NT)
    train_in = inn[0:slots].T
    for o in (keep, give):
        o[32:96, :] = train_in[:, 0:128]
        o[96:160, :] = train_in[:, 128:256]
    out = None
    for k in range(2):
        for c in groups[k + 1]:
            c.wait()
        cols = slice(half * k, half * (k + 1))
        term = mm(g_v[:, cols], po_v[:, cols], NT)
        out = term if out is None else out + term
    queries = jnp.concatenate([inn[slots:], out[slots:]], axis=1)
    out_t[...] = out[0:slots].T
    for core, o in enumerate((keep, give)):
        o[160:176, :] = queries
        for chip, at in enumerate((0, 176)):
            who = me ^ (core + 2 * chip)
            quarter = out_t[pl.ds(pl.multiple_of(who * 16, 16), 16), :]
            o[at : at + 16, :] = quarter[:, 0:128]
            o[at + 16 : at + 32, :] = quarter[:, 128:256]


def dot3(a, b, axis):
    ah, al = split(a)
    bh, bl = split(b)
    dims = NT if axis == 1 else TN
    return mm(jnp.concatenate([ah, ah, al], axis=axis), jnp.concatenate([bh, bl, bh], axis=axis), dims)


def features_kernel(tl, ql, mine, got, feats, scr, qscr):
    me = lax.axis_index("mp")
    lane = lax.broadcasted_iota(jnp.int32, (16, 128), 1)
    low = lax.broadcasted_iota(jnp.int32, (8, 128), 1) < 64
    for pair in range(2):
        out = mine[16 * pair : 16 * pair + 16] + got[144 + 16 * pair : 160 + 16 * pair]
        inn = mine[32 + 64 * pair : 96 + 64 * pair] + got[64 * pair : 64 * pair + 64]
        first = jnp.where(lane < jnp.minimum(tl[2 * pair], 64), out, 0.0)
        second = jnp.where((lane >= 64) & (lane < 64 + tl[2 * pair + 1]), out, 0.0)
        left = jnp.concatenate([first, second], axis=0)
        right = jnp.concatenate([inn, inn], axis=0)
        scr[32 * pair : 32 * pair + 32, :] = dot3(left, right, 1)
    for r in range(4):
        even = scr[pl.ds(16 * r, 8, stride=2), :]
        odd = scr[pl.ds(16 * r + 1, 8, stride=2), :]
        feats[8 * r : 8 * r + 8, :] = jnp.where(low, even, odd) * (1.0 / math.sqrt(LEN))
    q = mine[160:176] + got[128:144]
    slot = lax.broadcasted_iota(jnp.int32, (16, 64), 0)
    qin = q[:, 0:64]
    qout = q[:, 64:128]
    first = jnp.where(slot < ql[0], qout, 0.0)
    second = jnp.where((slot >= 8) & (slot < 8 + ql[1]), qout, 0.0)
    qscr[...] = dot3(jnp.concatenate([first, second], axis=1), jnp.concatenate([qin, qin], axis=1), 0)
    for r in range(2):
        scr[16 * r : 16 * r + 16, :] = qscr[pl.ds(pl.multiple_of(64 * r + me * 16, 16), 16), :]
    for r in range(2):
        even = scr[pl.ds(16 * r, 8, stride=2), :]
        odd = scr[pl.ds(16 * r + 1, 8, stride=2), :]
        feats[32 + 8 * r : 40 + 8 * r, :] = jnp.where(low, even, odd) * (1.0 / math.sqrt(QLEN))


def gram_kernel(tiles, part, xh_ref, xl_ref):
    for a in range(8):
        cols = [tiles[pl.ds(8 * r + a, 32, stride=48), :] for r in range(6)]
        high, low = split(jnp.concatenate(cols, axis=0))
        xh_ref[:, 128 * a : 128 * a + 128] = high
        xl_ref[:, 128 * a : 128 * a + 128] = low
    xh, xl = xh_ref[...], xl_ref[...]
    fh = xh[0:128]
    total = mm(xh, xh, NT) + mm(xh, xl, NT) + mm(xl, xh, NT)
    row = lax.broadcasted_iota(jnp.int32, (64, 64), 0)
    col = lax.broadcasted_iota(jnp.int32, (64, 64), 1)

    def diagonal(block):
        return jnp.sum(jnp.where(row == col, block, 0.0), axis=0, keepdims=True)

    first = total[0:64, 0:64]
    both = jnp.where(row >= col, total[64:128, 64:128], first)
    part[0:64, :] = jnp.concatenate([total[64:128, 0:64], both], axis=1)
    part[64:128, :] = jnp.concatenate([total[0:64, 128:192], total[64:128, 128:192]], axis=1)
    tail = jnp.concatenate([diagonal(total[128:192, 128:192]), diagonal(first)], axis=1)
    part[128:136, :] = jnp.broadcast_to(tail, (8, 128))


def solve_kernel(mine, got, xh, xl, precond, scores, ys, ts):
    dp = lax.axis_index("dp")
    me = lax.axis_index("mp")
    x = mine[...] + got[...]
    row = lax.broadcasted_iota(jnp.int32, (64, 64), 0)
    col = lax.broadcasted_iota(jnp.int32, (64, 64), 1)
    corner, both = x[0:64, 0:64], x[0:64, 64:128]
    flip = both.T
    diag = x[128:129, 64:128]
    upper = jnp.where(row < col, both, jnp.where(row > col, flip, diag))
    lower = jnp.where(row < col, flip, both)
    gram = jnp.concatenate(
        [jnp.concatenate([upper, corner.T], axis=1), jnp.concatenate([corner, lower], axis=1)],
        axis=0,
    )
    cross = jnp.concatenate([x[64:128, 0:64], x[64:128, 64:128]], axis=0)
    norm_q = x[128:129, 0:64]
    trace = jnp.sum(diag + jnp.sum(jnp.where(row == col, both, 0.0), axis=0, keepdims=True),
                    axis=1, keepdims=True)
    damp = trace * (DAMPING / (ROWS * RANK * RANK)) + EPSILON
    inv_rows = 1.0 / ROWS
    gh, gl = split(gram)
    stacked = jnp.concatenate([gh, gl], axis=0)

    def times_gram(y):
        yh, yl = split(y)
        t = mm(stacked, jnp.concatenate([yh, yl], axis=1), NN)
        t = t[0:128] + t[128:256]
        return t[:, 0:64] + t[:, 64:128]

    def total(v):
        return jnp.sum(v, axis=0, keepdims=True)

    def inner(alpha, w, y):
        return alpha * alpha * norm_q + total(w * (alpha * cross + y))

    ra, rw, ry = jnp.ones((1, 64), jnp.float32), jnp.zeros((128, 64), jnp.float32), cross
    da, dw, dy = ra, rw, ry
    za, zw, zy = jnp.zeros((1, 64), jnp.float32), rw, rw
    rr = norm_q
    dd = norm_q
    for step in range(ITERS):
        curvature = damp * dd + total(dy * dy) * inv_rows
        size = rr / curvature
        za, zw, zy = za + size * da, zw + size * dw, zy + size * dy
        if step == ITERS - 1:
            break
        iy = damp * dy + times_gram(dy) * inv_rows
        ra = ra - size * (damp * da)
        rw = rw - size * (damp * dw + dy * inv_rows)
        ry = ry - size * iy
        new = inner(ra, rw, ry)
        ratio = new / rr
        da, dw, dy = ra + ratio * da, rw + ratio * dw, ry + ratio * dy
        rr = new
        dd = inner(da, dw, dy)
    weights = jnp.concatenate([zw, jnp.where(row == col, za, 0.0)], axis=0)
    turned = weights.T
    pad = jnp.zeros((32, 64), jnp.float32)
    for k in range(2):
        turn = turned[32 * k : 32 * k + 32]
        ts[pl.ds(k, 32, stride=2), :] = turn[:, 0:128]
        ts[pl.ds(64 + k, 32, stride=2), :] = jnp.concatenate([turn[:, 128:192], pad], axis=1)
    wh, wl = split(jnp.concatenate([ts[0:64, :], ts[64:128, 0:64]], axis=1))
    ys[...] = jnp.concatenate([zy, jnp.zeros_like(zy)], axis=1)
    high = xh[...]
    z = mm(jnp.concatenate([wh, wl], axis=0), high, NN)
    precond[...] = z[0:64] + z[64:128] + mm(wh, xl[...], NN)
    mine_rows = ys[pl.ds(dp, 4, stride=32), :][:, 0:64]
    slot = lax.broadcasted_iota(jnp.int32, (64, 16), 0)
    want = lax.broadcasted_iota(jnp.int32, (64, 16), 1)
    pick = (slot == (want % 2) * 32 + 8 * me + want // 2).astype(jnp.float32)
    scores[...] = lax.dot_general(mine_rows, pick, NN, precision=lax.Precision.HIGHEST,
                                  preferred_element_type=jnp.float32)


def whole(n):
    return [pl.BlockSpec(memory_space=pltpu.VMEM)] * n


def call(kernel, shapes, in_specs, scratch, name):
    return pl.pallas_call(
        kernel,
        out_shape=[jax.ShapeDtypeStruct(s, t) for s, t in shapes],
        in_specs=in_specs,
        out_specs=whole(len(shapes)),
        scratch_shapes=scratch,
        compiler_params=pltpu.CompilerParams(vmem_limit_bytes=VMEM),
        name=name,
    )


def local(train_acts, train_grads, train_lengths, query_acts, query_grads, query_lengths,
          proj_in, proj_out):
    d, ff = proj_in.shape[1], proj_out.shape[1]
    bf, f32 = jnp.bfloat16, jnp.float32
    other_core = [(i, i ^ 1) for i in range(4)]
    other_chip = [(i, i ^ 2) for i in range(4)]
    keep, give = call(
        project_kernel,
        [((208, 128), f32)] * 2,
        [pl.BlockSpec(memory_space=pltpu.HBM)] * 6,
        [
            pltpu.VMEM((272, d), bf),
            pltpu.VMEM((272, ff), bf),
            pltpu.VMEM((64, d), bf),
            pltpu.VMEM((64, ff), bf),
            pltpu.VMEM((64, 256), f32),
            pltpu.SemaphoreType.DMA((18,)),
        ],
        "project",
    )(*(pltpu.with_memory_space_constraint(a, pltpu.HBM)
        for a in (train_acts, train_grads, query_acts.reshape(16, d),
                  query_grads.reshape(16, ff), proj_in, proj_out)))
    keep = keep + lax.ppermute(give, "mp", other_core)
    got = lax.ppermute(keep[32:], "mp", other_chip)
    smem = pl.BlockSpec(memory_space=pltpu.SMEM)
    (tiles,) = call(
        features_kernel,
        [((48, 128), f32)],
        [smem, smem] + whole(2),
        [pltpu.VMEM((64, 128), f32), pltpu.VMEM((128, 128), f32)],
        "features",
    )(train_lengths, query_lengths, keep, got)
    size = lax.axis_size("dp")
    tiles = lax.all_to_all(jnp.broadcast_to(tiles[None], (size, 48, 128)), "dp", 0, 0, tiled=True)
    part, xh, xl = call(
        gram_kernel,
        [((136, 128), f32), ((192, 1024), bf), ((192, 1024), bf)],
        whole(1),
        [],
        "gram",
    )(tiles.reshape(-1, 128))
    part = part + lax.ppermute(part, "mp", other_core)
    got = lax.ppermute(part, "mp", other_chip)
    precond, scores = call(
        solve_kernel,
        [((64, 1024), f32), ((4, 16), f32)],
        whole(4),
        [pltpu.VMEM((128, 128), f32)] * 2,
        "solve",
    )(part, got, xh, xl)
    return precond, scores


def solution(mesh):
    in_specs = (
        P("dp", None, "mp"),
        P("dp", None, "mp"),
        P("dp"),
        P("dp", None, "mp"),
        P("dp", None, "mp"),
        P("dp"),
        P(None, "mp"),
        P(None, "mp"),
    )
    out_specs = (P(None, "mp"), P("dp", "mp"))
    return jax.shard_map(local, mesh=mesh, in_specs=in_specs, out_specs=out_specs, check_vma=False)
```

```python
import math

import jax
import jax.numpy as jnp
from jax import lax
from jax.experimental import pallas as pl
from jax.experimental.pallas import tpu as pltpu
from jax.sharding import PartitionSpec as P

ITERS = 4
DAMPING = 0.5
EPSILON = 1e-06
ROWS, QUERIES, RANK, LEN, QLEN = 128, 64, 64, 64, 8
VMEM = 48 * 2**20

NT = (((1,), (1,)), ((), ()))
NN = (((1,), (0,)), ((), ()))
TN = (((0,), (0,)), ((), ()))


def mm(a, b, dims):
    return lax.dot_general(a, b, dims, preferred_element_type=jnp.float32)


def split(x):
    high = x.astype(jnp.bfloat16)
    return high, (x - high.astype(jnp.float32)).astype(jnp.bfloat16)


def project_kernel(tl, ql, ta, tg, qa, qg, pi, po, keep, give,
                   tl_s, ql_s, a_v, g_v, pi_v, po_v, out_t, sems):
    slots, ff = tg.shape
    bounds = (0, 1280, 2560, 3584)
    count = iter(range(32))

    def load(src, dst):
        return pltpu.make_async_copy(src, dst, sems.at[next(count)])

    groups = [[load(pi, pi_v), load(qa, a_v.at[slots : slots + 16]), load(ta, a_v.at[0:slots])]]
    for lo, hi in zip(bounds[:-1], bounds[1:]):
        cols = pl.ds(lo, hi - lo)
        groups.append([load(po.at[:, cols], po_v.at[:, cols]),
                       load(qg.at[:, cols], g_v.at[slots : slots + 16, cols]),
                       load(tg.at[:, cols], g_v.at[0:slots, cols])])
    groups.append([load(tl, tl_s), load(ql, ql_s)])
    for group in groups:
        for c in group:
            c.start()
    me = lax.axis_index("mp")
    for c in groups[0]:
        c.wait()
    inn = mm(a_v[...], pi_v[...], NT)
    train_in = inn[0:slots].T
    for o in (keep, give):
        o[32:96, :] = train_in[:, 0:128]
        o[96:160, :] = train_in[:, 128:256]
    out = None
    for k in range(len(bounds) - 1):
        for c in groups[k + 1]:
            c.wait()
        cols = slice(bounds[k], bounds[k + 1])
        term = mm(g_v[:, cols], po_v[:, cols], NT)
        out = term if out is None else out + term
    for c in groups[-1]:
        c.wait()
    slot = lax.broadcasted_iota(jnp.int32, (16, 64), 0)
    used = slot < jnp.minimum(ql_s[0], QLEN)
    used |= (slot >= QLEN) & (slot < QLEN + ql_s[1])
    queries = jnp.concatenate([inn[slots:], jnp.where(used, out[slots:], 0.0)], axis=1)
    lane = lax.broadcasted_iota(jnp.int32, (64, slots), 1)
    used = None
    for r in range(slots // LEN):
        own = (lane >= LEN * r) & (lane < LEN * r + jnp.minimum(tl_s[r], LEN))
        used = own if used is None else used | own
    out_t[...] = jnp.where(used, out[0:slots].T, 0.0)
    for core, o in enumerate((keep, give)):
        o[160:176, :] = queries
        for chip, at in enumerate((0, 176)):
            who = me ^ (core + 2 * chip)
            quarter = out_t[pl.ds(pl.multiple_of(who * 16, 16), 16), :]
            o[at : at + 16, :] = quarter[:, 0:128]
            o[at + 16 : at + 32, :] = quarter[:, 128:256]


def dot3(a, b, axis):
    ah, al = split(a)
    bh, bl = split(b)
    dims = NT if axis == 1 else TN
    return mm(jnp.concatenate([ah, ah, al], axis=axis), jnp.concatenate([bh, bl, bh], axis=axis), dims)


def features_kernel(mine, got, feats, scr, qscr):
    me = lax.axis_index("mp")
    left_lanes = lax.broadcasted_iota(jnp.int32, (16, 128), 1) < 64
    low = left_lanes[0:8]
    q = mine[160:176] + got[128:144]
    early = lax.broadcasted_iota(jnp.int32, (16, 64), 0) < QLEN
    qin, qout = q[:, 0:64], q[:, 64:128]
    left = jnp.concatenate([jnp.where(early, qout, 0.0), jnp.where(early, 0.0, qout)], axis=1)
    qscr[...] = dot3(left, jnp.concatenate([qin, qin], axis=1), 0)
    for pair in range(2):
        out = mine[16 * pair : 16 * pair + 16] + got[144 + 16 * pair : 160 + 16 * pair]
        inn = mine[32 + 64 * pair : 96 + 64 * pair] + got[64 * pair : 64 * pair + 64]
        left = jnp.concatenate([jnp.where(left_lanes, out, 0.0), jnp.where(left_lanes, 0.0, out)], axis=0)
        scr[32 * pair : 32 * pair + 32, :] = dot3(left, jnp.concatenate([inn, inn], axis=0), 1)
    for r in range(2):
        scr[64 + 16 * r : 80 + 16 * r, :] = qscr[pl.ds(pl.multiple_of(64 * r + me * 16, 16), 16), :]
    for r in range(6):
        even = scr[pl.ds(16 * r, 8, stride=2), :]
        odd = scr[pl.ds(16 * r + 1, 8, stride=2), :]
        scale = 1.0 / math.sqrt(LEN if r < 4 else QLEN)
        feats[8 * r : 8 * r + 8, :] = jnp.where(low, even, odd) * scale


def gram_kernel(tiles, part, xh_ref, xl_ref):
    squares = jnp.zeros((64, 128), jnp.float32)
    total = None
    for base in range(0, 8, 2):
        highs, lows = [], []
        for a in range(base, base + 2):
            x = jnp.concatenate([tiles[pl.ds(8 * r + a, 32, stride=48), :] for r in range(6)], axis=0)
            squares += x[128:192] * x[128:192]
            high, low = split(x)
            xh_ref[:, 128 * a : 128 * a + 128] = high
            xl_ref[:, 128 * a : 128 * a + 128] = low
            highs.append(high)
            lows.append(low)
        high = jnp.concatenate(highs, axis=1)
        low = jnp.concatenate(lows, axis=1)
        t = mm(jnp.concatenate([high[0:128], low[0:128]], axis=0), high, NT)
        term = t[0:128] + t[128:256] + mm(high[0:128], low, NT)
        total = term if total is None else total + term
    ones = jnp.ones((16, 128), jnp.bfloat16)
    high, low = split(squares)
    norms = mm(ones, high, NT) + mm(ones, low, NT)
    row = lax.broadcasted_iota(jnp.int32, (64, 64), 0)
    col = lax.broadcasted_iota(jnp.int32, (64, 64), 1)
    first = total[0:64, 0:64]
    both = jnp.where(row >= col, total[64:128, 64:128], first)
    part[0:64, :] = jnp.concatenate([total[64:128, 0:64], both], axis=1)
    part[64:128, :] = jnp.concatenate([total[0:64, 128:192], total[64:128, 128:192]], axis=1)
    diag = jnp.sum(jnp.where(row == col, first, 0.0), axis=0, keepdims=True)
    part[128:136, :] = jnp.concatenate([norms[0:8], jnp.broadcast_to(diag, (8, 64))], axis=1)


def solve_kernel(mine, got, xh, xl, precond, scores, ys, ts, zs, sems):
    dp = lax.axis_index("dp")
    me = lax.axis_index("mp")
    x = mine[...] + got[...]
    row = lax.broadcasted_iota(jnp.int32, (64, 64), 0)
    col = lax.broadcasted_iota(jnp.int32, (64, 64), 1)
    corner, both = x[0:64, 0:64], x[0:64, 64:128]
    flip = both.T
    diag = x[128:129, 64:128]
    upper = jnp.where(row < col, both, jnp.where(row > col, flip, diag))
    lower = jnp.where(row < col, flip, both)
    gram = jnp.concatenate(
        [jnp.concatenate([upper, corner.T], axis=1), jnp.concatenate([corner, lower], axis=1)],
        axis=0,
    )
    cross = jnp.concatenate([x[64:128, 0:64], x[64:128, 64:128]], axis=0)
    norm_q = x[128:129, 0:64]
    trace = jnp.sum(diag + jnp.sum(jnp.where(row == col, both, 0.0), axis=0, keepdims=True),
                    axis=1, keepdims=True)
    damp = trace * (DAMPING / (ROWS * RANK * RANK)) + EPSILON
    inv_rows = 1.0 / ROWS
    gh, gl = split(gram)
    spread = jnp.concatenate([gh, gl, gh], axis=1)

    def times_gram(y):
        yh, yl = split(y)
        return mm(spread, jnp.concatenate([yh, yh, yl], axis=0), NN)

    def total(v):
        return jnp.sum(v, axis=0, keepdims=True)

    def inner(alpha, w, y):
        return alpha * alpha * norm_q + total(w * (alpha * cross + y))

    rr = norm_q
    size = rr / (damp * rr + total(cross * cross) * inv_rows)
    za, zw, zy = size, jnp.zeros_like(cross), size * cross
    ra, rw = 1.0 - size * damp, (-inv_rows * size) * cross
    ry = cross - size * (damp * cross + times_gram(cross) * inv_rows)
    new = inner(ra, rw, ry)
    ratio = new / rr
    da, dw, dy = ra + ratio, rw, ry + ratio * cross
    for step in range(1, ITERS):
        rr = new
        curvature = damp * inner(da, dw, dy) + total(dy * dy) * inv_rows
        size = rr / curvature
        za, zw, zy = za + size * da, zw + size * dw, zy + size * dy
        if step == ITERS - 1:
            break
        iy = damp * dy + times_gram(dy) * inv_rows
        ra = ra - size * (damp * da)
        rw = rw - size * (damp * dw + dy * inv_rows)
        ry = ry - size * iy
        new = inner(ra, rw, ry)
        ratio = new / rr
        da, dw, dy = ra + ratio * da, rw + ratio * dw, ry + ratio * dy
    weights = jnp.concatenate([zw, jnp.where(row == col, za, 0.0)], axis=0)
    turned = weights.T
    pad = jnp.zeros((32, 64), jnp.float32)
    for k in range(2):
        turn = turned[32 * k : 32 * k + 32]
        ts[pl.ds(k, 32, stride=2), :] = turn[:, 0:128]
        ts[pl.ds(64 + k, 32, stride=2), :] = jnp.concatenate([turn[:, 128:192], pad], axis=1)
    wh, wl = split(jnp.concatenate([ts[0:64, :], ts[64:128, 0:64]], axis=1))
    ys[...] = jnp.concatenate([zy, jnp.zeros_like(zy)], axis=1)
    stacked = jnp.concatenate([wh, wl], axis=0)
    width = 512
    copies = []
    for c in range(2):
        cols = slice(width * c, width * (c + 1))
        z = mm(stacked, xh[:, cols], NN)
        precond[:, cols] = z[0:64] + z[64:128] + mm(wh, xl[:, cols], NN)
    mine_rows = ys[pl.ds(dp, 4, stride=32), :][:, 0:64]
    slot = lax.broadcasted_iota(jnp.int32, (64, 16), 0)
    want = lax.broadcasted_iota(jnp.int32, (64, 16), 1)
    pick = (slot == (want % 2) * 32 + 8 * me + want // 2).astype(jnp.float32)
    scores[...] = lax.dot_general(mine_rows, pick, NN, precision=lax.Precision.HIGHEST,
                                  preferred_element_type=jnp.float32)


def whole(n):
    return [pl.BlockSpec(memory_space=pltpu.VMEM)] * n


def call(kernel, shapes, in_specs, scratch, name, out_specs=None):
    return pl.pallas_call(
        kernel,
        out_shape=[jax.ShapeDtypeStruct(s, t) for s, t in shapes],
        in_specs=in_specs,
        out_specs=out_specs or whole(len(shapes)),
        scratch_shapes=scratch,
        compiler_params=pltpu.CompilerParams(vmem_limit_bytes=VMEM),
        name=name,
    )


def local(train_acts, train_grads, train_lengths, query_acts, query_grads, query_lengths,
          proj_in, proj_out):
    d, ff = proj_in.shape[1], proj_out.shape[1]
    bf, f32 = jnp.bfloat16, jnp.float32
    other_core = [(i, i ^ 1) for i in range(4)]
    other_chip = [(i, i ^ 2) for i in range(4)]
    keep, give = call(
        project_kernel,
        [((208, 128), f32)] * 2,
        [pl.BlockSpec(memory_space=pltpu.HBM)] * 8,
        [
            pltpu.SMEM((4,), jnp.int32),
            pltpu.SMEM((2,), jnp.int32),
            pltpu.VMEM((272, d), bf),
            pltpu.VMEM((272, ff), bf),
            pltpu.VMEM((64, d), bf),
            pltpu.VMEM((64, ff), bf),
            pltpu.VMEM((64, 256), f32),
            pltpu.SemaphoreType.DMA((18,)),
        ],
        "project",
    )(*(pltpu.with_memory_space_constraint(a, pltpu.HBM)
        for a in (train_lengths, query_lengths, train_acts.reshape(256, d), train_grads.reshape(256, ff), query_acts.reshape(16, d),
                  query_grads.reshape(16, ff), proj_in, proj_out)))
    keep = keep + lax.ppermute(give, "mp", other_core)
    got = lax.ppermute(keep[32:], "mp", other_chip)
    (tiles,) = call(
        features_kernel,
        [((48, 128), f32)],
        whole(2),
        [pltpu.VMEM((96, 128), f32), pltpu.VMEM((128, 128), f32)],
        "features",
    )(keep, got)
    size = lax.axis_size("dp")
    tiles = lax.all_to_all(jnp.broadcast_to(tiles[None], (size, 48, 128)), "dp", 0, 0, tiled=True)
    part, xh, xl = call(
        gram_kernel,
        [((136, 128), f32), ((192, 1024), bf), ((192, 1024), bf)],
        whole(1),
        [],
        "gram",
    )(tiles.reshape(-1, 128))
    part = part + lax.ppermute(part, "mp", other_core)
    got = lax.ppermute(part, "mp", other_chip)
    precond, scores = call(
        solve_kernel,
        [((64, 1024), f32), ((4, 16), f32)],
        whole(4),
        [pltpu.VMEM((128, 128), f32), pltpu.VMEM((128, 128), f32),
         pltpu.VMEM((64, 1024), f32), pltpu.SemaphoreType.DMA((2,))],
        "solve",
    )(part, got, xh, xl)
    return precond, scores


def solution(mesh):
    in_specs = (
        P("dp", None, "mp"),
        P("dp", None, "mp"),
        P("dp"),
        P("dp", None, "mp"),
        P("dp", None, "mp"),
        P("dp"),
        P(None, "mp"),
        P(None, "mp"),
    )
    out_specs = (P(None, "mp"), P("dp", "mp"))
    return jax.shard_map(local, mesh=mesh, in_specs=in_specs, out_specs=out_specs, check_vma=False)
```

```python
import math

import jax
import jax.numpy as jnp
from jax import lax
from jax.experimental import pallas as pl
from jax.experimental.pallas import tpu as pltpu
from jax.sharding import PartitionSpec as P

ITERS = 4
DAMPING = 0.5
EPSILON = 1e-06
ROWS, QUERIES, RANK, LEN, QLEN = 128, 64, 64, 64, 8
VMEM = 48 * 2**20

NT = (((1,), (1,)), ((), ()))
NN = (((1,), (0,)), ((), ()))
TN = (((0,), (0,)), ((), ()))


def mm(a, b, dims):
    return lax.dot_general(a, b, dims, preferred_element_type=jnp.float32)


def split(x):
    high = x.astype(jnp.bfloat16)
    return high, (x - high.astype(jnp.float32)).astype(jnp.bfloat16)


def project_kernel(tl, ql, ta, tg, qa, qg, pi, po, keep, give,
                   tl_s, ql_s, a_v, g_v, pi_v, po_v, out_t, sems):
    slots, ff = tg.shape
    bounds = (0, 1280, 2560, 3584)
    count = iter(range(32))

    def load(src, dst):
        return pltpu.make_async_copy(src, dst, sems.at[next(count)])

    groups = [[load(pi, pi_v), load(qa, a_v.at[slots : slots + 16]), load(ta, a_v.at[0:slots])]]
    for lo, hi in zip(bounds[:-1], bounds[1:]):
        cols = pl.ds(lo, hi - lo)
        groups.append([load(po.at[:, cols], po_v.at[:, cols]),
                       load(qg.at[:, cols], g_v.at[slots : slots + 16, cols]),
                       load(tg.at[:, cols], g_v.at[0:slots, cols])])
    groups.append([load(tl, tl_s), load(ql, ql_s)])
    for group in groups:
        for c in group:
            c.start()
    me = lax.axis_index("mp")
    for c in groups[0]:
        c.wait()
    inn = mm(a_v[...], pi_v[...], NT)
    train_in = inn[0:slots].T
    for o in (keep, give):
        o[32:96, :] = train_in[:, 0:128]
        o[96:160, :] = train_in[:, 128:256]
    out = None
    for k in range(len(bounds) - 1):
        for c in groups[k + 1]:
            c.wait()
        cols = slice(bounds[k], bounds[k + 1])
        term = mm(g_v[:, cols], po_v[:, cols], NT)
        out = term if out is None else out + term
    for c in groups[-1]:
        c.wait()
    slot = lax.broadcasted_iota(jnp.int32, (16, 64), 0)
    used = slot < jnp.minimum(ql_s[0], QLEN)
    used |= (slot >= QLEN) & (slot < QLEN + ql_s[1])
    queries = jnp.concatenate([inn[slots:], jnp.where(used, out[slots:], 0.0)], axis=1)
    lane = lax.broadcasted_iota(jnp.int32, (64, slots), 1)
    used = None
    for r in range(slots // LEN):
        own = (lane >= LEN * r) & (lane < LEN * r + jnp.minimum(tl_s[r], LEN))
        used = own if used is None else used | own
    out_t[...] = jnp.where(used, out[0:slots].T, 0.0)
    for core, o in enumerate((keep, give)):
        o[160:176, :] = queries
        for chip, at in enumerate((0, 176)):
            who = me ^ (core + 2 * chip)
            quarter = out_t[pl.ds(pl.multiple_of(who * 16, 16), 16), :]
            o[at : at + 16, :] = quarter[:, 0:128]
            o[at + 16 : at + 32, :] = quarter[:, 128:256]


def dot3(a, b, axis):
    ah, al = split(a)
    bh, bl = split(b)
    dims = NT if axis == 1 else TN
    return mm(jnp.concatenate([ah, ah, al], axis=axis), jnp.concatenate([bh, bl, bh], axis=axis), dims)


def features_kernel(mine, got, feats, scr, qscr):
    me = lax.axis_index("mp")
    left_lanes = lax.broadcasted_iota(jnp.int32, (16, 128), 1) < 64
    low = left_lanes[0:8]
    q = mine[160:176] + got[128:144]
    early = lax.broadcasted_iota(jnp.int32, (16, 64), 0) < QLEN
    qin, qout = q[:, 0:64], q[:, 64:128]
    left = jnp.concatenate([jnp.where(early, qout, 0.0), jnp.where(early, 0.0, qout)], axis=1)
    qscr[...] = dot3(left, jnp.concatenate([qin, qin], axis=1), 0)
    for pair in range(2):
        out = mine[16 * pair : 16 * pair + 16] + got[144 + 16 * pair : 160 + 16 * pair]
        inn = mine[32 + 64 * pair : 96 + 64 * pair] + got[64 * pair : 64 * pair + 64]
        left = jnp.concatenate([jnp.where(left_lanes, out, 0.0), jnp.where(left_lanes, 0.0, out)], axis=0)
        scr[32 * pair : 32 * pair + 32, :] = dot3(left, jnp.concatenate([inn, inn], axis=0), 1)
    for r in range(2):
        scr[64 + 16 * r : 80 + 16 * r, :] = qscr[pl.ds(pl.multiple_of(64 * r + me * 16, 16), 16), :]
    for r in range(6):
        even = scr[pl.ds(16 * r, 8, stride=2), :]
        odd = scr[pl.ds(16 * r + 1, 8, stride=2), :]
        scale = 1.0 / math.sqrt(LEN if r < 4 else QLEN)
        feats[8 * r : 8 * r + 8, :] = jnp.where(low, even, odd) * scale


def gram_kernel(tiles, part, xh_ref, xl_ref):
    planes = [tiles.at[pl.ds(384 * k, 384), :] for k in (0, 2, 1, 3)]
    squares = jnp.zeros((64, 128), jnp.float32)
    total = None
    for base in range(0, 8, 2):
        highs, lows = [], []
        for a in range(base, base + 2):
            x = jnp.concatenate(
                [p[pl.ds(8 * r + a, 8, stride=48), :] for r in range(6) for p in planes], axis=0
            )
            squares += x[128:192] * x[128:192]
            high, low = split(x)
            xh_ref[:, 128 * a : 128 * a + 128] = high
            xl_ref[:, 128 * a : 128 * a + 128] = low
            highs.append(high)
            lows.append(low)
        high = jnp.concatenate(highs, axis=1)
        low = jnp.concatenate(lows, axis=1)
        t = mm(jnp.concatenate([high[0:128], low[0:128]], axis=0), high, NT)
        term = t[0:128] + t[128:256] + mm(high[0:128], low, NT)
        total = term if total is None else total + term
    ones = jnp.ones((16, 128), jnp.bfloat16)
    high, low = split(squares)
    norms = mm(ones, high, NT) + mm(ones, low, NT)
    row = lax.broadcasted_iota(jnp.int32, (64, 64), 0)
    col = lax.broadcasted_iota(jnp.int32, (64, 64), 1)
    first = total[0:64, 0:64]
    both = jnp.where(row >= col, total[64:128, 64:128], first)
    part[0:64, :] = jnp.concatenate([total[64:128, 0:64], both], axis=1)
    part[64:128, :] = jnp.concatenate([total[0:64, 128:192], total[64:128, 128:192]], axis=1)
    diag = jnp.sum(jnp.where(row == col, first, 0.0), axis=0, keepdims=True)
    part[128:136, :] = jnp.concatenate([norms[0:8], jnp.broadcast_to(diag, (8, 64))], axis=1)


def query_at(i, dp):
    slot = i & 31
    back = (slot & 2) | ((slot >> 2) & 1)
    z = ((dp >> 3) - back) & 3
    y = (((dp >> 1) & 3) - (slot >> 3)) & 3
    x = (dp & 1) ^ (slot & 1)
    return 2 * (8 * z + 2 * y + x) + (i >> 5)


def solve_kernel(mine, got, xh, xl, precond, scores, ys):
    dp = lax.axis_index("dp")
    me = lax.axis_index("mp")
    x = mine[...] + got[...]
    row = lax.broadcasted_iota(jnp.int32, (64, 64), 0)
    col = lax.broadcasted_iota(jnp.int32, (64, 64), 1)
    corner, both = x[0:64, 0:64], x[0:64, 64:128]
    flip = both.T
    diag = x[128:129, 64:128]
    upper = jnp.where(row < col, both, jnp.where(row > col, flip, diag))
    lower = jnp.where(row < col, flip, both)
    gram = jnp.concatenate(
        [jnp.concatenate([upper, corner.T], axis=1), jnp.concatenate([corner, lower], axis=1)],
        axis=0,
    )
    cross = jnp.concatenate([x[64:128, 0:64], x[64:128, 64:128]], axis=0)
    norm_q = x[128:129, 0:64]
    trace = jnp.sum(diag + jnp.sum(jnp.where(row == col, both, 0.0), axis=0, keepdims=True),
                    axis=1, keepdims=True)
    damp = trace * (DAMPING / (ROWS * RANK * RANK)) + EPSILON
    inv_rows = 1.0 / ROWS
    gh, gl = split(gram)
    spread = jnp.concatenate([gh, gl, gh], axis=1)

    def times_gram(y):
        yh, yl = split(y)
        return mm(spread, jnp.concatenate([yh, yh, yl], axis=0), NN)

    def total(v):
        return jnp.sum(v, axis=0, keepdims=True)

    def inner(alpha, w, y):
        return alpha * alpha * norm_q + total(w * (alpha * cross + y))

    rr = norm_q
    size = rr / (damp * rr + total(cross * cross) * inv_rows)
    za, zw, zy = size, jnp.zeros_like(cross), size * cross
    ra, rw = 1.0 - size * damp, (-inv_rows * size) * cross
    ry = cross - size * (damp * cross + times_gram(cross) * inv_rows)
    new = inner(ra, rw, ry)
    ratio = new / rr
    da, dw, dy = ra + ratio, rw, ry + ratio * cross
    for step in range(1, ITERS):
        rr = new
        curvature = damp * inner(da, dw, dy) + total(dy * dy) * inv_rows
        size = rr / curvature
        za, zw, zy = za + size * da, zw + size * dw, zy + size * dy
        if step == ITERS - 1:
            break
        iy = damp * dy + times_gram(dy) * inv_rows
        ra = ra - size * (damp * da)
        rw = rw - size * (damp * dw + dy * inv_rows)
        ry = ry - size * iy
        new = inner(ra, rw, ry)
        ratio = new / rr
        da, dw, dy = ra + ratio * da, rw + ratio * dw, ry + ratio * dy
    weights = jnp.concatenate([zw, jnp.where(row == col, za, 0.0)], axis=0)
    place = query_at(lax.broadcasted_iota(jnp.int32, (64, 64), 1), dp)
    order = (place == row).astype(jnp.bfloat16)
    wh, wl = (mm(order, w, NT).astype(jnp.bfloat16) for w in split(weights))
    ys[...] = jnp.concatenate([zy, jnp.zeros_like(zy)], axis=1)
    stacked = jnp.concatenate([wh, wl], axis=0)
    width = 512
    for c in range(2):
        cols = slice(width * c, width * (c + 1))
        z = mm(stacked, xh[:, cols], NN)
        precond[:, cols] = z[0:64] + z[64:128] + mm(wh, xl[:, cols], NN)
    mine_rows = ys[pl.ds(0, 4, stride=32), :][:, 0:64]
    place = query_at(lax.broadcasted_iota(jnp.int32, (64, 16), 0), dp)
    want = 16 * me + lax.broadcasted_iota(jnp.int32, (64, 16), 1)
    pick = (place == want).astype(jnp.float32)
    scores[...] = lax.dot_general(mine_rows, pick, NN, precision=lax.Precision.HIGHEST,
                                  preferred_element_type=jnp.float32)


def whole(n):
    return [pl.BlockSpec(memory_space=pltpu.VMEM)] * n


def call(kernel, shapes, in_specs, scratch, name, out_specs=None):
    return pl.pallas_call(
        kernel,
        out_shape=[jax.ShapeDtypeStruct(s, t) for s, t in shapes],
        in_specs=in_specs,
        out_specs=out_specs or whole(len(shapes)),
        scratch_shapes=scratch,
        compiler_params=pltpu.CompilerParams(vmem_limit_bytes=VMEM),
        name=name,
    )


def shifts(array, step, size):
    pieces = {0: array}
    for k in (2, 1, 3) if size == 4 else (1,):
        pairs = []
        for i in range(32):
            z, y, x = i >> 3, (i >> 1) & 3, i & 1
            for _ in range(k):
                z, y, x = step(z, y, x)
            pairs.append((i, 8 * z + 2 * y + x))
        pieces[k] = lax.ppermute(array, "dp", pairs)
    return [pieces[k] for k in range(size)]


def local(train_acts, train_grads, train_lengths, query_acts, query_grads, query_lengths,
          proj_in, proj_out):
    d, ff = proj_in.shape[1], proj_out.shape[1]
    bf, f32 = jnp.bfloat16, jnp.float32
    other_core = [(i, i ^ 1) for i in range(4)]
    other_chip = [(i, i ^ 2) for i in range(4)]
    keep, give = call(
        project_kernel,
        [((208, 128), f32)] * 2,
        [pl.BlockSpec(memory_space=pltpu.HBM)] * 8,
        [
            pltpu.SMEM((4,), jnp.int32),
            pltpu.SMEM((2,), jnp.int32),
            pltpu.VMEM((272, d), bf),
            pltpu.VMEM((272, ff), bf),
            pltpu.VMEM((64, d), bf),
            pltpu.VMEM((64, ff), bf),
            pltpu.VMEM((64, 256), f32),
            pltpu.SemaphoreType.DMA((18,)),
        ],
        "project",
    )(*(pltpu.with_memory_space_constraint(a, pltpu.HBM)
        for a in (train_lengths, query_lengths, train_acts.reshape(256, d), train_grads.reshape(256, ff), query_acts.reshape(16, d),
                  query_grads.reshape(16, ff), proj_in, proj_out)))
    keep = keep + lax.ppermute(give, "mp", other_core)
    got = lax.ppermute(keep[32:], "mp", other_chip)
    (tiles,) = call(
        features_kernel,
        [((48, 128), f32)],
        whole(2),
        [pltpu.VMEM((96, 128), f32), pltpu.VMEM((128, 128), f32)],
        "features",
    )(keep, got)
    tiles = jnp.concatenate(shifts(tiles, lambda z, y, x: (z, y, x ^ 1), 2), axis=0)
    t0, t1, t2, t3 = shifts(tiles, lambda z, y, x: ((z + 1) % 4, y, x), 4)
    tiles = jnp.concatenate([t0, t2, t1, t3], axis=0)
    p0, p1, p2, p3 = shifts(tiles, lambda z, y, x: (z, (y + 1) % 4, x), 4)
    tiles = jnp.concatenate([p0, p2, p1, p3], axis=0)
    part, xh, xl = call(
        gram_kernel,
        [((136, 128), f32), ((192, 1024), bf), ((192, 1024), bf)],
        whole(1),
        [],
        "gram",
    )(tiles)
    part = part + lax.ppermute(part, "mp", other_core)
    got = lax.ppermute(part, "mp", other_chip)
    precond, scores = call(
        solve_kernel,
        [((64, 1024), f32), ((4, 16), f32)],
        whole(4),
        [pltpu.VMEM((128, 128), f32)],
        "solve",
    )(part, got, xh, xl)
    return precond, scores


def solution(mesh):
    in_specs = (
        P("dp", None, "mp"),
        P("dp", None, "mp"),
        P("dp"),
        P("dp", None, "mp"),
        P("dp", None, "mp"),
        P("dp"),
        P(None, "mp"),
        P(None, "mp"),
    )
    out_specs = (P(None, "mp"), P("dp", "mp"))
    return jax.shard_map(local, mesh=mesh, in_specs=in_specs, out_specs=out_specs, check_vma=False)
```

```python
import math

import jax
import jax.numpy as jnp
from jax import lax
from jax.experimental import pallas as pl
from jax.experimental.pallas import tpu as pltpu
from jax.sharding import PartitionSpec as P

ITERS = 4
DAMPING = 0.5
EPSILON = 1e-06
ROWS, QUERIES, RANK, LEN, QLEN = 128, 64, 64, 64, 8
VMEM = 48 * 2**20

NT = (((1,), (1,)), ((), ()))
NN = (((1,), (0,)), ((), ()))
TN = (((0,), (0,)), ((), ()))


def mm(a, b, dims):
    return lax.dot_general(a, b, dims, preferred_element_type=jnp.float32)


def split(x):
    high = x.astype(jnp.bfloat16)
    return high, (x - high.astype(jnp.float32)).astype(jnp.bfloat16)


def project_kernel(tl, ql, ta, tg, qa, qg, pi, po, keep, give,
                   tl_s, ql_s, a_v, g_v, pi_v, po_v, out_t, sems):
    slots, ff = tg.shape
    bounds = (0, 1280, 2560, 3584)
    count = iter(range(32))

    def load(src, dst):
        return pltpu.make_async_copy(src, dst, sems.at[next(count)])

    groups = [[load(pi, pi_v), load(qa, a_v.at[slots : slots + 16]), load(ta.at[0:128], a_v.at[0:128]),
               load(ta.at[128:256], a_v.at[128:256])]]
    for lo, hi in zip(bounds[:-1], bounds[1:]):
        cols = pl.ds(lo, hi - lo)
        groups.append([load(po.at[:, cols], po_v.at[:, cols]),
                       load(qg.at[:, cols], g_v.at[slots : slots + 16, cols]),
                       load(tg.at[0:128, cols], g_v.at[0:128, cols]),
                       load(tg.at[128:256, cols], g_v.at[128:256, cols])])
    groups.append([load(tl, tl_s), load(ql, ql_s)])
    for group in groups:
        for c in group:
            c.start()
    me = lax.axis_index("mp")
    for c in groups[0]:
        c.wait()
    inn = mm(a_v[...], pi_v[...], NT)
    train_in = inn[0:slots].T
    for o in (keep, give):
        o[32:96, :] = train_in[:, 0:128]
        o[96:160, :] = train_in[:, 128:256]
    out = None
    for k in range(len(bounds) - 1):
        for c in groups[k + 1]:
            c.wait()
        cols = slice(bounds[k], bounds[k + 1])
        term = mm(g_v[:, cols], po_v[:, cols], NT)
        out = term if out is None else out + term
    for c in groups[-1]:
        c.wait()
    slot = lax.broadcasted_iota(jnp.int32, (16, 64), 0)
    used = slot < jnp.minimum(ql_s[0], QLEN)
    used |= (slot >= QLEN) & (slot < QLEN + ql_s[1])
    queries = jnp.concatenate([inn[slots:], jnp.where(used, out[slots:], 0.0)], axis=1)
    lane = lax.broadcasted_iota(jnp.int32, (64, slots), 1)
    used = None
    for r in range(slots // LEN):
        own = (lane >= LEN * r) & (lane < LEN * r + jnp.minimum(tl_s[r], LEN))
        used = own if used is None else used | own
    out_t[...] = jnp.where(used, out[0:slots].T, 0.0)
    for core, o in enumerate((keep, give)):
        o[160:176, :] = queries
        for chip, at in enumerate((0, 176)):
            who = me ^ (core + 2 * chip)
            quarter = out_t[pl.ds(pl.multiple_of(who * 16, 16), 16), :]
            o[at : at + 16, :] = quarter[:, 0:128]
            o[at + 16 : at + 32, :] = quarter[:, 128:256]


def dot3(a, b, axis):
    ah, al = split(a)
    bh, bl = split(b)
    dims = NT if axis == 1 else TN
    return mm(jnp.concatenate([ah, ah, al], axis=axis), jnp.concatenate([bh, bl, bh], axis=axis), dims)


def features_kernel(mine, got, feats, scr, qscr):
    me = lax.axis_index("mp")
    left_lanes = lax.broadcasted_iota(jnp.int32, (16, 128), 1) < 64
    low = left_lanes[0:8]
    q = mine[160:176] + got[128:144]
    early = lax.broadcasted_iota(jnp.int32, (16, 64), 0) < QLEN
    qin, qout = q[:, 0:64], q[:, 64:128]
    left = jnp.concatenate([jnp.where(early, qout, 0.0), jnp.where(early, 0.0, qout)], axis=1)
    qscr[...] = dot3(left, jnp.concatenate([qin, qin], axis=1), 0)
    for pair in range(2):
        out = mine[16 * pair : 16 * pair + 16] + got[144 + 16 * pair : 160 + 16 * pair]
        inn = mine[32 + 64 * pair : 96 + 64 * pair] + got[64 * pair : 64 * pair + 64]
        left = jnp.concatenate([jnp.where(left_lanes, out, 0.0), jnp.where(left_lanes, 0.0, out)], axis=0)
        scr[32 * pair : 32 * pair + 32, :] = dot3(left, jnp.concatenate([inn, inn], axis=0), 1)
    for r in range(2):
        scr[64 + 16 * r : 80 + 16 * r, :] = qscr[pl.ds(pl.multiple_of(64 * r + me * 16, 16), 16), :]
    for r in range(6):
        even = scr[pl.ds(16 * r, 8, stride=2), :]
        odd = scr[pl.ds(16 * r + 1, 8, stride=2), :]
        scale = 1.0 / math.sqrt(LEN if r < 4 else QLEN)
        feats[8 * r : 8 * r + 8, :] = jnp.where(low, even, odd) * scale


def gram_kernel(tiles, part, xh_ref, xl_ref):
    planes = [tiles.at[pl.ds(384 * k, 384), :] for k in (0, 2, 1, 3)]
    squares = jnp.zeros((64, 128), jnp.float32)
    total = None
    for base in range(0, 8, 2):
        highs, lows = [], []
        for a in range(base, base + 2):
            x = jnp.concatenate(
                [p[pl.ds(8 * r + a, 8, stride=48), :] for r in range(6) for p in planes], axis=0
            )
            squares += x[128:192] * x[128:192]
            high, low = split(x)
            xh_ref[:, 128 * a : 128 * a + 128] = high
            xl_ref[:, 128 * a : 128 * a + 128] = low
            highs.append(high)
            lows.append(low)
        high = jnp.concatenate(highs, axis=1)
        low = jnp.concatenate(lows, axis=1)
        t = mm(jnp.concatenate([high[0:128], low[0:128]], axis=0), high, NT)
        term = t[0:128] + t[128:256] + mm(high[0:128], low, NT)
        total = term if total is None else total + term
    ones = jnp.ones((16, 128), jnp.bfloat16)
    high, low = split(squares)
    norms = mm(ones, high, NT) + mm(ones, low, NT)
    row = lax.broadcasted_iota(jnp.int32, (64, 64), 0)
    col = lax.broadcasted_iota(jnp.int32, (64, 64), 1)
    first = total[0:64, 0:64]
    both = jnp.where(row >= col, total[64:128, 64:128], first)
    part[0:64, :] = jnp.concatenate([total[64:128, 0:64], both], axis=1)
    part[64:128, :] = jnp.concatenate([total[0:64, 128:192], total[64:128, 128:192]], axis=1)
    diag = jnp.sum(jnp.where(row == col, first, 0.0), axis=0, keepdims=True)
    part[128:136, :] = jnp.concatenate([norms[0:8], jnp.broadcast_to(diag, (8, 64))], axis=1)


def query_at(i, dp):
    slot = i & 31
    back = (slot & 2) | ((slot >> 2) & 1)
    z = ((dp >> 3) - back) & 3
    y = (((dp >> 1) & 3) - (slot >> 3)) & 3
    x = (dp & 1) ^ (slot & 1)
    return 2 * (8 * z + 2 * y + x) + (i >> 5)


def solve_kernel(mine, got, xh, xl, precond, scores, ys):
    dp = lax.axis_index("dp")
    me = lax.axis_index("mp")
    x = mine[...] + got[...]
    row = lax.broadcasted_iota(jnp.int32, (64, 64), 0)
    col = lax.broadcasted_iota(jnp.int32, (64, 64), 1)
    corner, both = x[0:64, 0:64], x[0:64, 64:128]
    flip = both.T
    diag = x[128:129, 64:128]
    upper = jnp.where(row < col, both, jnp.where(row > col, flip, diag))
    lower = jnp.where(row < col, flip, both)
    gram = jnp.concatenate(
        [jnp.concatenate([upper, corner.T], axis=1), jnp.concatenate([corner, lower], axis=1)],
        axis=0,
    )
    cross = jnp.concatenate([x[64:128, 0:64], x[64:128, 64:128]], axis=0)
    norm_q = x[128:129, 0:64]
    trace = jnp.sum(diag + jnp.sum(jnp.where(row == col, both, 0.0), axis=0, keepdims=True),
                    axis=1, keepdims=True)
    damp = trace * (DAMPING / (ROWS * RANK * RANK)) + EPSILON
    inv_rows = 1.0 / ROWS
    gh, gl = split(gram)
    spread = jnp.concatenate([gh, gl, gh], axis=1)

    def times_gram(y):
        yh, yl = split(y)
        return mm(spread, jnp.concatenate([yh, yh, yl], axis=0), NN)

    def total(v):
        return jnp.sum(v, axis=0, keepdims=True)

    def inner(alpha, w, y):
        return alpha * alpha * norm_q + total(w * (alpha * cross + y))

    rr = norm_q
    size = rr / (damp * rr + total(cross * cross) * inv_rows)
    za, zw, zy = size, jnp.zeros_like(cross), size * cross
    ra, rw = 1.0 - size * damp, (-inv_rows * size) * cross
    ry = cross - size * (damp * cross + times_gram(cross) * inv_rows)
    new = inner(ra, rw, ry)
    ratio = new / rr
    da, dw, dy = ra + ratio, rw, ry + ratio * cross
    for step in range(1, ITERS):
        rr = new
        curvature = damp * inner(da, dw, dy) + total(dy * dy) * inv_rows
        size = rr / curvature
        za, zw, zy = za + size * da, zw + size * dw, zy + size * dy
        if step == ITERS - 1:
            break
        iy = damp * dy + times_gram(dy) * inv_rows
        ra = ra - size * (damp * da)
        rw = rw - size * (damp * dw + dy * inv_rows)
        ry = ry - size * iy
        new = inner(ra, rw, ry)
        ratio = new / rr
        da, dw, dy = ra + ratio * da, rw + ratio * dw, ry + ratio * dy
    weights = jnp.concatenate([zw, jnp.where(row == col, za, 0.0)], axis=0)
    place = query_at(lax.broadcasted_iota(jnp.int32, (64, 64), 1), dp)
    order = (place == row).astype(jnp.bfloat16)
    wh, wl = (mm(order, w, NT).astype(jnp.bfloat16) for w in split(weights))
    ys[...] = jnp.concatenate([zy, jnp.zeros_like(zy)], axis=1)
    stacked = jnp.concatenate([wh, wl], axis=0)
    width = 512
    for c in range(2):
        cols = slice(width * c, width * (c + 1))
        z = mm(stacked, xh[:, cols], NN)
        precond[:, cols] = z[0:64] + z[64:128] + mm(wh, xl[:, cols], NN)
    mine_rows = ys[pl.ds(0, 4, stride=32), :][:, 0:64]
    place = query_at(lax.broadcasted_iota(jnp.int32, (64, 16), 0), dp)
    want = 16 * me + lax.broadcasted_iota(jnp.int32, (64, 16), 1)
    pick = (place == want).astype(jnp.float32)
    scores[...] = lax.dot_general(mine_rows, pick, NN, precision=lax.Precision.HIGHEST,
                                  preferred_element_type=jnp.float32)


def whole(n):
    return [pl.BlockSpec(memory_space=pltpu.VMEM)] * n


def call(kernel, shapes, in_specs, scratch, name, out_specs=None):
    return pl.pallas_call(
        kernel,
        out_shape=[jax.ShapeDtypeStruct(s, t) for s, t in shapes],
        in_specs=in_specs,
        out_specs=out_specs or whole(len(shapes)),
        scratch_shapes=scratch,
        compiler_params=pltpu.CompilerParams(vmem_limit_bytes=VMEM),
        name=name,
    )


def shifts(array, step, size):
    pieces = {0: array}
    for k in (2, 1, 3) if size == 4 else (1,):
        pairs = []
        for i in range(32):
            z, y, x = i >> 3, (i >> 1) & 3, i & 1
            for _ in range(k):
                z, y, x = step(z, y, x)
            pairs.append((i, 8 * z + 2 * y + x))
        pieces[k] = lax.ppermute(array, "dp", pairs)
    return [pieces[k] for k in range(size)]


def local(train_acts, train_grads, train_lengths, query_acts, query_grads, query_lengths,
          proj_in, proj_out):
    d, ff = proj_in.shape[1], proj_out.shape[1]
    bf, f32 = jnp.bfloat16, jnp.float32
    other_core = [(i, i ^ 1) for i in range(4)]
    other_chip = [(i, i ^ 2) for i in range(4)]
    keep, give = call(
        project_kernel,
        [((208, 128), f32)] * 2,
        [pl.BlockSpec(memory_space=pltpu.HBM)] * 8,
        [
            pltpu.SMEM((4,), jnp.int32),
            pltpu.SMEM((2,), jnp.int32),
            pltpu.VMEM((272, d), bf),
            pltpu.VMEM((272, ff), bf),
            pltpu.VMEM((64, d), bf),
            pltpu.VMEM((64, ff), bf),
            pltpu.VMEM((64, 256), f32),
            pltpu.SemaphoreType.DMA((18,)),
        ],
        "project",
    )(*(pltpu.with_memory_space_constraint(a, pltpu.HBM)
        for a in (train_lengths, query_lengths, train_acts.reshape(256, d), train_grads.reshape(256, ff), query_acts.reshape(16, d),
                  query_grads.reshape(16, ff), proj_in, proj_out)))
    keep = keep + lax.ppermute(give, "mp", other_core)
    got = lax.ppermute(keep[32:], "mp", other_chip)
    (tiles,) = call(
        features_kernel,
        [((48, 128), f32)],
        whole(2),
        [pltpu.VMEM((96, 128), f32), pltpu.VMEM((128, 128), f32)],
        "features",
    )(keep, got)
    tiles = jnp.concatenate(shifts(tiles, lambda z, y, x: (z, y, x ^ 1), 2), axis=0)
    t0, t1, t2, t3 = shifts(tiles, lambda z, y, x: ((z + 1) % 4, y, x), 4)
    tiles = jnp.concatenate([t0, t2, t1, t3], axis=0)
    p0, p1, p2, p3 = shifts(tiles, lambda z, y, x: (z, (y + 1) % 4, x), 4)
    tiles = jnp.concatenate([p0, p2, p1, p3], axis=0)
    part, xh, xl = call(
        gram_kernel,
        [((136, 128), f32), ((192, 1024), bf), ((192, 1024), bf)],
        whole(1),
        [],
        "gram",
    )(tiles)
    part = part + lax.ppermute(part, "mp", other_core)
    got = lax.ppermute(part, "mp", other_chip)
    precond, scores = call(
        solve_kernel,
        [((64, 1024), f32), ((4, 16), f32)],
        whole(4),
        [pltpu.VMEM((128, 128), f32)],
        "solve",
    )(part, got, xh, xl)
    return precond, scores


def solution(mesh):
    in_specs = (
        P("dp", None, "mp"),
        P("dp", None, "mp"),
        P("dp"),
        P("dp", None, "mp"),
        P("dp", None, "mp"),
        P("dp"),
        P(None, "mp"),
        P(None, "mp"),
    )
    out_specs = (P(None, "mp"), P("dp", "mp"))
    return jax.shard_map(local, mesh=mesh, in_specs=in_specs, out_specs=out_specs, check_vma=False)
```
